32 devices in a mesh: groups: 2 (over y), expert: 4 (over x, core), seq: 4 (over z).
Axes of the slice: x: 2, y: 2, z: 4, core: 2. Of those that a mesh axis runs over, the one named last changes fastest.
Arguments:
- tokens: bfloat16 [1024, 7168], P(('groups', 'seq'), 'expert'), parts along dimension 0, may hold values from -6 to 6
- out_grad: bfloat16 [1024, 7168], P(('groups', 'seq'), 'expert'), parts along dimension 0, may hold values from -3 to 3
- routes: int32 [1024, 8], P('groups'), parts along dimension 0, may hold values from 0 to 15, all different within a row; in each aligned block of 128 rows (0 to 127, 128 to 255, ...) at most 80 rows name the same one
- route_weights: float32 [1024, 8], P('groups'), parts along dimension 0, may hold values from 0.05 to 0.5
- w_gate: bfloat16 [16, 7168, 1024], P('expert', None, 'seq'), may hold values from -0.0625 to 0.0625
- w_up: bfloat16 [16, 7168, 1024], P('expert', None, 'seq'), may hold values from -0.0625 to 0.0625
- w_down: bfloat16 [16, 1024, 7168], P('expert', 'seq'), may hold values from -0.1875 to 0.1875
Outputs:
- token_grad: bfloat16 [1024, 7168], P(('groups', 'seq'), 'expert'), parts along dimension 0
- weight_grad_gate: bfloat16 [32, 7168, 1024], P(('groups', 'expert'), None, 'seq'), parts along dimension 0
- weight_grad_up: bfloat16 [32, 7168, 1024], P(('groups', 'expert'), None, 'seq'), parts along dimension 0
- weight_grad_down: bfloat16 [32, 1024, 7168], P(('groups', 'expert'), 'seq'), parts along dimension 0
- gate_grad: float32 [1024, 8], P(('groups', 'seq')), parts along dimension 0
The draws below stay inside these ranges and needn't reach their ends.
There are 2 independent parts, one for each index of `groups`. The reference program is written for one: setup_inputs(seed, part) draws one part's arguments, and reference() takes and returns one part's arrays. A program takes and returns all parts, laid end to end along the dimension named above; an argument that names none is the same for every part. Nothing has to cross between parts.
Inputs may be any that keep to these rules, and one draw needn't show every extreme that they name: `routes`: each row names 8 different experts. In each aligned block of 128 rows no expert is named by more than 80 rows, a bound that some block reaches.
All inputs are finite; a program needn't handle non-finite values.
Results may differ from the reference program's by a relative error of at most 0.012.
Values may be sent and summed in bfloat16 or wider, within the bound.
A program may use at most 384 MiB of HBM per device.

```python
import math
import jax
import jax.numpy as jnp
import numpy as np
from jax import lax

D = 7168
H = 1024
EXPERTS = 16
TOPK = 8
TOK_DEV = 128
CAP = 80
TOKENS = 512
N_SEQ = 4


def levels(stream_key, shape, split, smallest, top_value):
    def one(axis_at, parts):
        heights = jax.random.uniform(jax.random.fold_in(jax.random.fold_in(stream_key, 6), axis_at), (parts,), jnp.float32, smallest / len(split), top_value / len(split))
        return jnp.repeat(jnp.exp(heights), shape[axis_at] // parts).reshape((-1,) + (1,) * (len(shape) - axis_at - 1))

    factor_of = one(*split[0])
    for cut in split[1:]:
        factor_of = factor_of * one(*cut)
    return factor_of


def assign_block(own_key, own, number, rows, amount, top, reach, lean):
    order = jax.random.permutation(own_key, amount)
    packed, ordinary = shares(amount, rows * top, reach, lean, True), shares(amount, rows * top, reach, lean, False)
    places = jnp.arange(amount)

    def named(tallies, turn):
        used = int((tallies > 0).sum())
        fixed = max(1, used // 4)
        shifted = fixed + (places - fixed + turn * (used - fixed)) % max(1, amount - fixed)
        return jnp.zeros((amount,), jnp.int32).at[order[jnp.where(places < fixed, places, shifted)]].set(jnp.asarray(tallies, jnp.int32))

    tallies = jnp.where(number % 4 == 0, named(packed, number // 4), named(ordinary, number - number // 4 - 1))
    mixed = jax.random.permutation(jax.random.fold_in(own, 3), amount)
    donor, receiver = mixed[0:amount // 2 * 2:2], mixed[1:amount // 2 * 2:2]
    room = jnp.minimum(tallies[donor] - 1, reach - tallies[receiver]) // 2
    room = jnp.where((donor == order[0]) | (receiver == order[0]) | (tallies[receiver] == 0), 0, jnp.maximum(room, 0))
    shifted = jax.random.randint(jax.random.fold_in(own, 4), (amount // 2,), 0, 1 << 20) % (room + 1)
    tallies = tallies.at[donor].add(-shifted).at[receiver].add(shifted)
    labels = jnp.searchsorted(jnp.cumsum(tallies), jnp.arange(rows * top), side="right").astype(jnp.int32)
    grid = labels.reshape(top, rows).T
    grid = grid[jax.random.permutation(jax.random.fold_in(own, 1), rows)]
    turn = jax.random.randint(jax.random.fold_in(own, 2), (rows, 1), 0, top)
    return jnp.take_along_axis(grid, (jnp.arange(top)[None, :] + turn) % top, axis=1)


def shares(count, total, reach, slope, full):
    weights = [(1 << 20) // math.isqrt(rank ** slope) + 1 for rank in range(1, count + 1)]
    largest = reach if full else min(reach, max(-(-total // count), total * weights[0] // sum(weights)))
    least = 1 if total - largest >= count - 1 else 0
    given, spare = [largest] + [least] * (count - 1), total - largest - least * (count - 1)
    while spare > 0:
        movable = [i for i in range(1, count) if given[i] < largest] or [i for i in range(1, count) if given[i] < reach]
        pool, remaining = sum([weights[i] for i in movable]), spare
        for i in movable:
            more = min(reach - given[i], max(1, remaining * weights[i] // pool), spare)
            given[i] = given[i] + more
            spare = spare - more
    return np.array(given)


def centred(key, shape, deviation, reach, cuts=(), kind=jnp.bfloat16):
    gain = levels(key, shape, cuts, -0.22, 0.18) if cuts else 1.0
    entries = jax.random.normal(key, shape, jnp.float32) * deviation * gain
    return jnp.minimum(jnp.maximum(entries, -reach), reach).astype(kind)


def setup_inputs(seed: int = 0, part: int = 0) -> dict:
    arg_keys = jax.random.split(jax.random.key(seed), 8)
    part_keys = jax.random.split(jax.random.fold_in(arg_keys[7], part), 8)
    tokens = centred(part_keys[0], (TOKENS, D), 1.0, 6.0, ((0, 4), (1, 4)))
    out_grad = centred(part_keys[1], (TOKENS, D), 0.5, 3.0, ((0, 4), (1, 4)))
    routes_keys = jax.random.split(jax.random.fold_in(part_keys[2], 1), TOKENS // TOK_DEV)
    routes_turns = jax.random.permutation(jax.random.fold_in(part_keys[2], 3), TOKENS // TOK_DEV)
    routes = jax.vmap(lambda own, number: assign_block(jax.random.fold_in(part_keys[2], 2), own, number, TOK_DEV, EXPERTS, TOPK, CAP, 2))(routes_keys, routes_turns).reshape((TOKENS, TOPK))
    route_weights = jnp.clip(jnp.exp(jax.random.uniform(part_keys[3], (TOKENS, TOPK), jnp.float32, math.log(0.05), math.log(0.5))), 0.05, 0.5)
    w_gate = centred(arg_keys[4], (EXPERTS, D, H), D ** -0.5, 0.0625, ((0, 4), (2, 4)))
    w_up = centred(arg_keys[5], (EXPERTS, D, H), D ** -0.5, 0.0625, ((0, 4), (2, 4)))
    w_down = centred(arg_keys[6], (EXPERTS, H, D), H ** -0.5, 0.1875, ((0, 4), (1, 4)))
    return {"tokens": tokens, "out_grad": out_grad, "routes": routes, "route_weights": route_weights, "w_gate": w_gate, "w_up": w_up, "w_down": w_down}


def slot_tables(shard_routes, shard_weights):
    shard_rows = shard_routes.shape[0]
    expert_ids = jnp.arange(EXPERTS, dtype=jnp.int32)
    hit_table = (shard_routes[:, :, None] == expert_ids[None, None, :]).astype(jnp.int32)
    member_of = jnp.sum(hit_table, axis=1)
    ranked = jnp.cumsum(member_of, axis=0) - member_of
    slot_ids = jnp.arange(CAP, dtype=jnp.int32)
    placed = member_of[:, :, None] * (ranked[:, :, None] == slot_ids[None, None, :]).astype(jnp.int32)
    row_ids = jnp.arange(shard_rows, dtype=jnp.int32)
    filled = jnp.sum(placed, axis=0)
    source = jnp.sum(placed * row_ids[:, None, None], axis=0) + (1 - filled) * shard_rows
    slot_of = jnp.sum(hit_table * ranked[:, None, :], axis=2)
    per_expert = jnp.sum(hit_table.astype(jnp.float32) * shard_weights[:, :, None], axis=1)
    slot_weight = jnp.sum(placed.astype(jnp.float32) * per_expert[:, :, None], axis=0)
    return source, slot_of, slot_weight


def reference(tokens, out_grad, routes, route_weights, w_gate, w_up, w_down):
    shard_routes = routes.reshape(N_SEQ, TOK_DEV, TOPK)
    source, slot_of, slot_weight = jax.vmap(slot_tables)(shard_routes, route_weights.reshape(N_SEQ, TOK_DEV, TOPK))
    slot_rows = N_SEQ * CAP
    offsets = (jnp.arange(N_SEQ, dtype=jnp.int32) * TOK_DEV)[:, None, None]
    pick_rows = jnp.where(source < TOK_DEV, source + offsets, TOKENS).astype(jnp.int32)
    pick_rows = jnp.transpose(pick_rows, (1, 0, 2)).reshape(EXPERTS, slot_rows)
    row_weight = jnp.transpose(slot_weight, (1, 0, 2)).reshape(EXPERTS, slot_rows)
    padded_tokens = jnp.concatenate([tokens, jnp.zeros((1, D), tokens.dtype)], 0)
    padded_grads = jnp.concatenate([out_grad, jnp.zeros((1, D), out_grad.dtype)], 0)
    block_width = H // N_SEQ

    def one_expert(items):
        gate_w, up_w, down_w, rows, weight = items
        rows_in = padded_tokens[rows]
        grads_in = padded_grads[rows]
        pre_gate = jnp.dot(rows_in, gate_w, preferred_element_type=jnp.float32)
        pre_up = jnp.dot(rows_in, up_w, preferred_element_type=jnp.float32)
        sigmoid_gate = jax.nn.sigmoid(pre_gate)
        activated = pre_gate * sigmoid_gate * pre_up
        back_grad = jnp.dot(grads_in, down_w.T, preferred_element_type=jnp.float32)
        scores = jnp.sum(activated * back_grad, axis=1)
        scaled = weight[:, None] * back_grad
        up_grad = (scaled * pre_gate * sigmoid_gate).astype(jnp.bfloat16)
        pre_grad = (scaled * pre_up * sigmoid_gate * (1.0 + pre_gate * (1.0 - sigmoid_gate))).astype(jnp.bfloat16)
        scaled_act = (weight[:, None] * activated).astype(jnp.bfloat16)
        grad_down = jnp.dot(scaled_act.T, grads_in, preferred_element_type=jnp.float32).astype(jnp.bfloat16)
        grad_gate = jnp.dot(rows_in.T, pre_grad, preferred_element_type=jnp.float32).astype(jnp.bfloat16)
        grad_up = jnp.dot(rows_in.T, up_grad, preferred_element_type=jnp.float32).astype(jnp.bfloat16)
        block_terms = jnp.einsum("zjh,djh->jzd", pre_grad.astype(jnp.float32).reshape(slot_rows, N_SEQ, block_width), gate_w.astype(jnp.float32).reshape(D, N_SEQ, block_width))
        block_terms = block_terms + jnp.einsum("zjh,djh->jzd", up_grad.astype(jnp.float32).reshape(slot_rows, N_SEQ, block_width), up_w.astype(jnp.float32).reshape(D, N_SEQ, block_width))
        rounded = lax.optimization_barrier(block_terms.astype(jnp.bfloat16))
        row_grads = jnp.sum(rounded.astype(jnp.float32), axis=0)
        return grad_gate, grad_up, grad_down, row_grads, scores

    grad_gate, grad_up, grad_down, row_grads, scores = lax.map(one_expert, (w_gate, w_up, w_down, pick_rows, row_weight))
    segment_start = (jnp.arange(N_SEQ, dtype=jnp.int32) * CAP)[:, None, None]
    row_index = (shard_routes * slot_rows + segment_start + slot_of).astype(jnp.int32).reshape(TOKENS, TOPK)
    flat_rows = row_grads.reshape(EXPERTS * slot_rows, D)
    token_sum = jnp.zeros((TOKENS, D), jnp.float32)
    for column in range(TOPK):
        token_sum = token_sum + flat_rows[row_index[:, column]]
    gate_grad = scores.reshape(EXPERTS * slot_rows)[row_index]
    return token_sum.astype(jnp.bfloat16), grad_gate, grad_up, grad_down, gate_grad
```

```python
import functools

import jax
import jax.numpy as jnp
from jax import lax
from jax.experimental import pallas as pl
from jax.experimental.pallas import tpu as pltpu
from jax.sharding import PartitionSpec as P

BOTH = ("expert", "seq")
VMEM_BYTES = 56 * 1024 * 1024
BF16 = jnp.bfloat16
F32 = jnp.float32


def params(dims):
    return pltpu.CompilerParams(
        vmem_limit_bytes=VMEM_BYTES, dimension_semantics=("arbitrary",) * dims
    )


def cost(flops, moved):
    return pl.CostEstimate(flops=int(flops), bytes_accessed=int(moved), transcendentals=0)


def dot_nn(a, b):
    return lax.dot_general(a, b, (((1,), (0,)), ((), ())), preferred_element_type=F32)


def dot_nt(a, b):
    return lax.dot_general(a, b, (((1,), (1,)), ((), ())), preferred_element_type=F32)


def pre_kernel(x_ref, gate_ref, up_ref, pre_gate_ref, pre_up_ref):
    c, block = pl.program_id(0), pl.program_id(1)
    group = gate_ref.shape[0]
    for i in range(group):
        e = block * group + i
        new_gate = dot_nn(x_ref[0], gate_ref[i])
        new_up = dot_nn(x_ref[0], up_ref[i])

        @pl.when(c == 0)
        def _():
            pre_gate_ref[e] = new_gate
            pre_up_ref[e] = new_up

        @pl.when(c > 0)
        def _():
            pre_gate_ref[e] += new_gate
            pre_up_ref[e] += new_up


def pre_products(x_all, w_gate, w_up):
    chunks, rows, features = x_all.shape
    experts, depth, width = w_gate.shape
    group = min(2, experts)
    weight_spec = pl.BlockSpec((group, features, width), lambda c, b: (b, c, 0))
    whole = pl.BlockSpec((experts, rows, width), lambda c, b: (0, 0, 0))
    out = jax.ShapeDtypeStruct((experts, rows, width), F32)
    return pl.pallas_call(
        pre_kernel,
        grid=(chunks, experts // group),
        in_specs=[
            pl.BlockSpec((1, rows, features), lambda c, b: (c, 0, 0)),
            weight_spec,
            weight_spec,
        ],
        out_specs=[whole, whole],
        out_shape=[out, out],
        compiler_params=params(2),
        cost_estimate=cost(
            4 * rows * depth * width * experts,
            2 * rows * depth + 4 * experts * depth * width + 8 * experts * rows * width,
        ),
        name="pre_products",
    )(x_all, w_gate, w_up)


def back_kernel(
    g_ref, down_ref, pre_gate_ref, pre_up_ref, weight_ref,
    grads_ref, scaled_act_ref, scores_ref, back_ref,
):
    c, block = pl.program_id(0), pl.program_id(1)
    last = pl.num_programs(0) - 1
    group, width = down_ref.shape[0], down_ref.shape[1]
    experts = back_ref.shape[0]
    for i in range(group):
        e = block * group + i
        new = dot_nt(g_ref[0], down_ref[i])

        @pl.when(c == 0)
        def _():
            back_ref[e] = new

        @pl.when(c > 0)
        def _():
            back_ref[e] += new

    @pl.when((c == last) & (block == pl.num_programs(1) - 1))
    def _():
        for e in range(experts):
            pre_gate = pre_gate_ref[e]
            pre_up = pre_up_ref[e]
            back = back_ref[e]
            r = weight_ref[:, e : e + 1]
            sig = jax.nn.sigmoid(pre_gate)
            silu = pre_gate * sig
            act = silu * pre_up
            scores_ref[:, e : e + 1] = jnp.sum(act * back, axis=1, keepdims=True)
            scaled = r * back
            grads_ref[:, e * width : (e + 1) * width] = (
                scaled * pre_up * sig * (1.0 + pre_gate * (1.0 - sig))
            ).astype(BF16)
            at = (experts + e) * width
            grads_ref[:, at : at + width] = (scaled * silu).astype(BF16)
            scaled_act_ref[e * width : (e + 1) * width, :] = (r * act).T.astype(BF16)


def back_products(g_all, w_down, pre_gate, pre_up, weight):
    chunks, rows, features = g_all.shape
    experts, width, depth = w_down.shape
    group = min(2, experts)
    whole = pl.BlockSpec((experts, rows, width), lambda c, b: (0, 0, 0))
    return pl.pallas_call(
        back_kernel,
        grid=(chunks, experts // group),
        in_specs=[
            pl.BlockSpec((1, rows, features), lambda c, b: (c, 0, 0)),
            pl.BlockSpec((group, width, features), lambda c, b: (b, 0, c)),
            whole,
            whole,
            pl.BlockSpec((rows, experts), lambda c, b: (0, 0)),
        ],
        out_specs=[
            pl.BlockSpec((rows, 2 * experts * width), lambda c, b: (0, 0)),
            pl.BlockSpec((experts * width, rows), lambda c, b: (0, 0)),
            pl.BlockSpec((rows, experts), lambda c, b: (0, 0)),
        ],
        out_shape=[
            jax.ShapeDtypeStruct((rows, 2 * experts * width), BF16),
            jax.ShapeDtypeStruct((experts * width, rows), BF16),
            jax.ShapeDtypeStruct((rows, experts), F32),
        ],
        scratch_shapes=[pltpu.VMEM((experts, rows, width), F32)],
        compiler_params=params(2),
        cost_estimate=cost(
            2 * rows * depth * width * experts,
            2 * rows * depth + 2 * experts * depth * width + 8 * experts * rows * width,
        ),
        name="back_products",
    )(g_all, w_down, pre_gate, pre_up, weight)


def row_kernel(grads_ref, gate_ref, up_ref, out_ref):
    experts, _, width = gate_ref.shape
    total = None
    for e in range(experts):
        for half, ref in enumerate((gate_ref, up_ref)):
            at = (half * experts + e) * width
            term = dot_nt(grads_ref[:, at : at + width], ref[e])
            total = term if total is None else total + term
    out_ref[0] = total.astype(BF16)


def row_products(grads, w_gate, w_up, chunks, steps, first, count):
    rows = grads.shape[0]
    experts, depth, width = w_gate.shape
    features = depth // chunks
    cut = count // steps
    weight_spec = pl.BlockSpec(
        (experts, cut, width), lambda c, n: (0, c * (features // cut) + first // cut + n, 0)
    )
    return pl.pallas_call(
        row_kernel,
        grid=(chunks, steps),
        in_specs=[
            pl.BlockSpec(grads.shape, lambda c, n: (0, 0)),
            weight_spec,
            weight_spec,
        ],
        out_specs=pl.BlockSpec((1, rows, cut), lambda c, n: (c, 0, n)),
        out_shape=jax.ShapeDtypeStruct((chunks, rows, count), BF16),
        compiler_params=params(2),
        cost_estimate=cost(
            4 * rows * chunks * count * width * experts,
            2 * rows * chunks * count + 4 * experts * chunks * count * width,
        ),
        name="row_products",
    )(grads, w_gate, w_up)


def weight_kernel(x_ref, g_ref, grads_ref, act_ref, gate_ref, up_ref, down_ref):
    experts, _, width = gate_ref.shape
    x_t = x_ref[0].T
    for e in range(experts):
        gate_ref[e] = dot_nn(x_t, grads_ref[:, e * width : (e + 1) * width]).astype(BF16)
        at = (experts + e) * width
        up_ref[e] = dot_nn(x_t, grads_ref[:, at : at + width]).astype(BF16)
        down_ref[e] = dot_nn(act_ref[e * width : (e + 1) * width, :], g_ref[0]).astype(BF16)


def weight_products(x_all, g_all, grads, act_t, experts, steps):
    chunks, rows, features = x_all.shape
    width = act_t.shape[0] // experts
    depth = chunks * features
    cut = features // steps
    token_spec = pl.BlockSpec((1, rows, cut), lambda c, n: (c, 0, n))
    tall = pl.BlockSpec((experts, cut, width), lambda c, n: (0, c * steps + n, 0))
    return pl.pallas_call(
        weight_kernel,
        grid=(chunks, steps),
        in_specs=[
            token_spec,
            token_spec,
            pl.BlockSpec(grads.shape, lambda c, n: (0, 0)),
            pl.BlockSpec(act_t.shape, lambda c, n: (0, 0)),
        ],
        out_specs=[
            tall,
            tall,
            pl.BlockSpec((experts, width, cut), lambda c, n: (0, 0, c * steps + n)),
        ],
        out_shape=[
            jax.ShapeDtypeStruct((experts, depth, width), BF16),
            jax.ShapeDtypeStruct((experts, depth, width), BF16),
            jax.ShapeDtypeStruct((experts, width, depth), BF16),
        ],
        compiler_params=params(2),
        cost_estimate=cost(
            6 * rows * depth * width * experts,
            4 * rows * depth + 6 * experts * depth * width,
        ),
        name="weight_products",
    )(x_all, g_all, grads, act_t)


def body(tokens, out_grad, routes, route_weights, w_gate, w_up, w_down):
    shards = lax.axis_size("seq")
    feature_shards = lax.axis_size("expert")
    tok_rows, features = tokens.shape
    rows = shards * tok_rows
    local_experts, depth, width = w_gate.shape
    first_expert = lax.axis_index("expert") * local_experts

    x_all = lax.all_gather(tokens, BOTH, axis=0, tiled=False).reshape(
        feature_shards, rows, features
    )
    g_all = lax.all_gather(out_grad, BOTH, axis=0, tiled=False).reshape(
        feature_shards, rows, features
    )
    local_ids = first_expert + jnp.arange(local_experts, dtype=jnp.int32)
    hit = routes[:, :, None] == local_ids[None, None, :]
    weight = jnp.sum(jnp.where(hit, route_weights[:, :, None], 0.0), axis=1)

    if features % 256 == 0:
        pre_gate, pre_up = pre_products(x_all, w_gate, w_up)
        grads, act_t, scores = back_products(g_all, w_down, pre_gate, pre_up, weight)
        part = row_products(grads, w_gate, w_up, feature_shards, 2, 0, features)
        weight_grads = lambda: weight_products(x_all, g_all, grads, act_t, local_experts, 2)
    else:
        part, scores, weight_grads = plain(x_all, g_all, weight, w_gate, w_up, w_down)

    part = part.reshape(feature_shards * shards, tok_rows, features)
    token_grad = lax.psum_scatter(part, BOTH, scatter_dimension=0, tiled=True)[0]
    picked = jnp.sum(jnp.where(hit, scores[:, None, :], 0.0), axis=2)
    gate_grad = lax.psum(lax.psum_scatter(picked, "seq", scatter_dimension=0, tiled=True), "expert")
    grad_gate, grad_up, grad_down = weight_grads()
    return token_grad, grad_gate, grad_up, grad_down, gate_grad


def plain(x_all, g_all, weight, w_gate, w_up, w_down):
    chunks, rows, features = x_all.shape
    experts, depth, width = w_gate.shape
    weight = weight.T[:, :, None]
    gate4 = w_gate.reshape(experts, chunks, features, width)
    up4 = w_up.reshape(experts, chunks, features, width)
    down4 = w_down.reshape(experts, width, chunks, features)
    einsum = functools.partial(jnp.einsum, preferred_element_type=F32)
    pre_gate = einsum("crf,ecfh->erh", x_all, gate4)
    pre_up = einsum("crf,ecfh->erh", x_all, up4)
    back = einsum("crf,ehcf->erh", g_all, down4)
    sig = jax.nn.sigmoid(pre_gate)
    act = pre_gate * sig * pre_up
    scores = jnp.sum(act * back, axis=2).T
    scaled = weight * back
    up_grad = (scaled * pre_gate * sig).astype(BF16)
    pre_grad = (scaled * pre_up * sig * (1.0 + pre_gate * (1.0 - sig))).astype(BF16)
    scaled_act = (weight * act).astype(BF16)
    part = einsum("erh,ecfh->crf", pre_grad, gate4) + einsum("erh,ecfh->crf", up_grad, up4)

    def weight_grads():
        return (
            einsum("crf,erh->ecfh", x_all, pre_grad).astype(BF16).reshape(w_gate.shape),
            einsum("crf,erh->ecfh", x_all, up_grad).astype(BF16).reshape(w_up.shape),
            einsum("erh,crf->ehcf", scaled_act, g_all).astype(BF16).reshape(w_down.shape),
        )

    return part.astype(BF16), scores, weight_grads


def solution(mesh):
    in_specs = (
        P(("groups", "seq"), "expert"),
        P(("groups", "seq"), "expert"),
        P("groups", None),
        P("groups", None),
        P("expert", None, "seq"),
        P("expert", None, "seq"),
        P("expert", "seq", None),
    )
    out_specs = (
        P(("groups", "seq"), "expert"),
        P(("groups", "expert"), None, "seq"),
        P(("groups", "expert"), None, "seq"),
        P(("groups", "expert"), "seq", None),
        P(("groups", "seq"), None),
    )
    return jax.shard_map(body, mesh=mesh, in_specs=in_specs, out_specs=out_specs, check_vma=False)
```

```python
import functools

import jax
import jax.numpy as jnp
from jax import lax
from jax.experimental import pallas as pl
from jax.experimental.pallas import tpu as pltpu
from jax.sharding import PartitionSpec as P

BOTH = ("expert", "seq")
VMEM_BYTES = 56 * 1024 * 1024
BF16 = jnp.bfloat16
F32 = jnp.float32


def params(dims):
    return pltpu.CompilerParams(
        vmem_limit_bytes=VMEM_BYTES, dimension_semantics=("arbitrary",) * dims
    )


def cost(flops, moved):
    return pl.CostEstimate(flops=int(flops), bytes_accessed=int(moved), transcendentals=0)


def dot_nn(a, b):
    return lax.dot_general(a, b, (((1,), (0,)), ((), ())), preferred_element_type=F32)


def dot_nt(a, b):
    return lax.dot_general(a, b, (((1,), (1,)), ((), ())), preferred_element_type=F32)


def forward_kernel(
    tokens_ref, grad_ref, gate_ref, up_ref, down_ref, weight_ref,
    x_all_ref, g_all_ref, grads_ref, scaled_act_ref, scores_ref,
    pre_gate_ref, pre_up_ref, back_ref,
    z_send, z_recv, x_send, x_recv, s_send, s_recv, local_sem,
):
    shards = lax.axis_size("seq")
    z = lax.axis_index("seq")
    me = lax.axis_index("expert")
    sib = me + 1 - 2 * lax.rem(me, 2)
    partner = lax.rem(me + 2, 4)
    far = lax.rem(sib + 2, 4)
    tok_rows, features = tokens_ref.shape
    experts, _, width = gate_ref.shape
    own_refs = (tokens_ref, grad_ref)
    all_refs = (x_all_ref, g_all_ref)

    def place(t, chunk, shard):
        return all_refs[t].at[chunk, pl.ds(pl.multiple_of(shard * tok_rows, tok_rows), tok_rows)]

    def remote(src, dst, send, recv, device):
        return pltpu.make_async_remote_copy(
            src_ref=src, dst_ref=dst, send_sem=send, recv_sem=recv,
            device_id=device, device_id_type=pl.DeviceIdType.MESH,
        )

    def source(t, chunk, d):
        return own_refs[t] if (d == 0 and chunk is me) else place(t, chunk, back_by(d))

    def back_by(d):
        return lax.rem(z + shards - d, shards)

    def z_copy(t, d):
        peer = lax.rem(z + d, shards)
        return remote(own_refs[t], place(t, me, z), z_send.at[t, d], z_recv.at[t, d], {"seq": peer})

    def x_copy(t, d):
        return remote(
            source(t, me, d), place(t, me, back_by(d)), x_send.at[t, d], x_recv.at[t, d],
            {"expert": partner},
        )

    def s_copy(t, which, d):
        chunk = (me, partner)[which]
        at = which * shards + d
        return remote(
            source(t, chunk, d), place(t, chunk, back_by(d)), s_send.at[t, at], s_recv.at[t, at],
            {"expert": sib},
        )

    def local(t):
        return pltpu.make_async_copy(own_refs[t], place(t, me, z), local_sem.at[t])

    barrier = pltpu.get_barrier_semaphore()
    for device in [{"expert": sib}, {"expert": partner}] + [
        {"seq": lax.rem(z + d, shards)} for d in range(1, shards)
    ]:
        pl.semaphore_signal(barrier, inc=1, device_id=device, device_id_type=pl.DeviceIdType.MESH)
    pl.semaphore_wait(barrier, shards + 1)

    group = 2 if experts % 2 == 0 else 1
    rows = shards * tok_rows

    def multiply_tokens(chunk, first):
        def step(x_ref, g_ref, u_ref):
            block = pl.program_id(0)
            for i in range(group):
                e = block * group + i
                new_gate = dot_nn(x_ref[...], g_ref[i])
                new_up = dot_nn(x_ref[...], u_ref[i])
                if first:
                    pre_gate_ref[e] = new_gate
                    pre_up_ref[e] = new_up
                else:
                    pre_gate_ref[e] += new_gate
                    pre_up_ref[e] += new_up

        weights = pl.BlockSpec((group, features, width), lambda b: (b, 0, 0))
        at = pl.ds(pl.multiple_of(chunk * features, features), features)
        pltpu.emit_pipeline(
            step,
            grid=(experts // group,),
            in_specs=[pl.BlockSpec((rows, features), lambda b: (0, 0)), weights, weights],
            out_specs=[],
        )(x_all_ref.at[chunk], gate_ref.at[:, at], up_ref.at[:, at])

    def multiply_grads(chunk, first):
        def step(g_ref, d_ref):
            block = pl.program_id(0)
            for i in range(group):
                e = block * group + i
                new = dot_nt(g_ref[...], d_ref[i])
                if first:
                    back_ref[e] = new
                else:
                    back_ref[e] += new

        at = pl.ds(pl.multiple_of(chunk * features, features), features)
        pltpu.emit_pipeline(
            step,
            grid=(experts // group,),
            in_specs=[
                pl.BlockSpec((rows, features), lambda b: (0, 0)),
                pl.BlockSpec((group, width, features), lambda b: (b, 0, 0)),
            ],
            out_specs=[],
        )(g_all_ref.at[chunk], down_ref.at[:, :, at])

    every = range(shards)
    others = range(1, shards)
    for d in others:
        z_copy(0, d).start()
    x_copy(0, 0).start()
    s_copy(0, 0, 0).start()
    x_copy(1, 0).start()
    local(0).start()
    local(1).start()
    for d in others:
        z_copy(0, d).wait_recv()
        x_copy(0, d).start()
        s_copy(0, 0, d).start()
    for d in others:
        z_copy(1, d).start()
    s_copy(1, 0, 0).start()
    local(0).wait()
    local(1).wait()
    multiply_tokens(me, True)
    for d in every:
        s_copy(0, 0, d).wait_recv()
    multiply_tokens(sib, False)
    for d in every:
        x_copy(0, d).wait_recv()
        s_copy(0, 1, d).start()
    multiply_tokens(partner, False)
    for d in every:
        s_copy(0, 1, d).wait_recv()
    multiply_tokens(far, False)
    for d in others:
        z_copy(1, d).wait_recv()
        x_copy(1, d).start()
        s_copy(1, 0, d).start()
    multiply_grads(me, True)
    for d in every:
        s_copy(1, 0, d).wait_recv()
    multiply_grads(sib, False)
    for d in every:
        x_copy(1, d).wait_recv()
        s_copy(1, 1, d).start()
    multiply_grads(partner, False)
    for d in every:
        s_copy(1, 1, d).wait_recv()
    multiply_grads(far, False)

    for e in range(experts):
        pre_gate = pre_gate_ref[e]
        pre_up = pre_up_ref[e]
        back = back_ref[e]
        r = weight_ref[:, e : e + 1]
        sig = jax.nn.sigmoid(pre_gate)
        silu = pre_gate * sig
        act = silu * pre_up
        scores_ref[:, e : e + 1] = jnp.sum(act * back, axis=1, keepdims=True)
        scaled = r * back
        grads_ref[:, e * width : (e + 1) * width] = (
            scaled * pre_up * sig * (1.0 + pre_gate * (1.0 - sig))
        ).astype(BF16)
        at = (experts + e) * width
        grads_ref[:, at : at + width] = (scaled * silu).astype(BF16)
        scaled_act_ref[e * width : (e + 1) * width, :] = (r * act).T.astype(BF16)

    for t in range(2):
        for d in others:
            z_copy(t, d).wait_send()
        for d in every:
            x_copy(t, d).wait_send()
            s_copy(t, 0, d).wait_send()
            s_copy(t, 1, d).wait_send()


def forward(tokens, out_grad, w_gate, w_up, w_down, weight, shards, chunks):
    tok_rows, features = tokens.shape
    rows = shards * tok_rows
    experts, depth, width = w_gate.shape
    any_spec = pl.BlockSpec(memory_space=pl.ANY)
    vmem_spec = pl.BlockSpec(memory_space=pltpu.VMEM)
    gathered = jax.ShapeDtypeStruct((chunks, rows, features), BF16)
    total = pltpu.VMEM((experts, rows, width), F32)
    dma = pltpu.SemaphoreType.DMA
    return pl.pallas_call(
        forward_kernel,
        in_specs=[any_spec] * 5 + [vmem_spec],
        out_specs=[any_spec] * 2 + [vmem_spec] * 3,
        out_shape=[
            gathered,
            gathered,
            jax.ShapeDtypeStruct((rows, 2 * experts * width), BF16),
            jax.ShapeDtypeStruct((experts * width, rows), BF16),
            jax.ShapeDtypeStruct((rows, experts), F32),
        ],
        scratch_shapes=[
            total,
            total,
            total,
            dma((2, shards)),
            dma((2, shards)),
            dma((2, shards)),
            dma((2, shards)),
            dma((2, 2 * shards)),
            dma((2, 2 * shards)),
            dma((2,)),
        ],
        compiler_params=pltpu.CompilerParams(
            vmem_limit_bytes=VMEM_BYTES, collective_id=0, has_side_effects=True
        ),
        cost_estimate=cost(
            6 * rows * depth * width * experts,
            8 * rows * depth + 6 * experts * depth * width,
        ),
        name="forward",
    )(tokens, out_grad, w_gate, w_up, w_down, weight)


def row_kernel(grads_ref, gate_ref, up_ref, out_ref):
    experts, _, width = gate_ref.shape
    total = None
    for e in range(experts):
        for half, ref in enumerate((gate_ref, up_ref)):
            at = (half * experts + e) * width
            term = dot_nt(grads_ref[:, at : at + width], ref[e])
            total = term if total is None else total + term
    out_ref[0] = total.astype(BF16)


def row_products(grads, w_gate, w_up, chunks, steps, first, count):
    rows = grads.shape[0]
    experts, depth, width = w_gate.shape
    features = depth // chunks
    cut = count // steps
    weight_spec = pl.BlockSpec(
        (experts, cut, width), lambda c, n: (0, c * (features // cut) + first // cut + n, 0)
    )
    return pl.pallas_call(
        row_kernel,
        grid=(chunks, steps),
        in_specs=[
            pl.BlockSpec(grads.shape, lambda c, n: (0, 0)),
            weight_spec,
            weight_spec,
        ],
        out_specs=pl.BlockSpec((1, rows, cut), lambda c, n: (c, 0, n)),
        out_shape=jax.ShapeDtypeStruct((chunks, rows, count), BF16),
        compiler_params=params(2),
        cost_estimate=cost(
            4 * rows * chunks * count * width * experts,
            2 * rows * chunks * count + 4 * experts * chunks * count * width,
        ),
        name="row_products",
    )(grads, w_gate, w_up)


def weight_kernel(x_ref, g_ref, grads_ref, act_ref, gate_ref, up_ref, down_ref):
    experts, _, width = gate_ref.shape
    x_t = x_ref[0].T
    for e in range(experts):
        gate_ref[e] = dot_nn(x_t, grads_ref[:, e * width : (e + 1) * width]).astype(BF16)
        at = (experts + e) * width
        up_ref[e] = dot_nn(x_t, grads_ref[:, at : at + width]).astype(BF16)
        down_ref[e] = dot_nn(act_ref[e * width : (e + 1) * width, :], g_ref[0]).astype(BF16)


def weight_products(x_all, g_all, grads, act_t, experts, steps):
    chunks, rows, features = x_all.shape
    width = act_t.shape[0] // experts
    depth = chunks * features
    cut = features // steps
    token_spec = pl.BlockSpec((1, rows, cut), lambda c, n: (c, 0, n))
    tall = pl.BlockSpec((experts, cut, width), lambda c, n: (0, c * steps + n, 0))
    return pl.pallas_call(
        weight_kernel,
        grid=(chunks, steps),
        in_specs=[
            token_spec,
            token_spec,
            pl.BlockSpec(grads.shape, lambda c, n: (0, 0)),
            pl.BlockSpec(act_t.shape, lambda c, n: (0, 0)),
        ],
        out_specs=[
            tall,
            tall,
            pl.BlockSpec((experts, width, cut), lambda c, n: (0, 0, c * steps + n)),
        ],
        out_shape=[
            jax.ShapeDtypeStruct((experts, depth, width), BF16),
            jax.ShapeDtypeStruct((experts, depth, width), BF16),
            jax.ShapeDtypeStruct((experts, width, depth), BF16),
        ],
        compiler_params=params(2),
        cost_estimate=cost(
            6 * rows * depth * width * experts,
            4 * rows * depth + 6 * experts * depth * width,
        ),
        name="weight_products",
    )(x_all, g_all, grads, act_t)


def body(tokens, out_grad, routes, route_weights, w_gate, w_up, w_down):
    shards = lax.axis_size("seq")
    feature_shards = lax.axis_size("expert")
    tok_rows, features = tokens.shape
    rows = shards * tok_rows
    local_experts, depth, width = w_gate.shape
    first_expert = lax.axis_index("expert") * local_experts

    local_ids = first_expert + jnp.arange(local_experts, dtype=jnp.int32)
    hit = routes[:, :, None] == local_ids[None, None, :]
    weight = jnp.sum(jnp.where(hit, route_weights[:, :, None], 0.0), axis=1)

    if feature_shards == 4 and features % 256 == 0:
        x_all, g_all, grads, act_t, scores = forward(
            tokens, out_grad, w_gate, w_up, w_down, weight, shards, feature_shards
        )
        part = row_products(grads, w_gate, w_up, feature_shards, 2, 0, features)
        weight_grads = lambda: weight_products(x_all, g_all, grads, act_t, local_experts, 2)
    else:
        x_all = lax.all_gather(tokens, BOTH, axis=0, tiled=False)
        g_all = lax.all_gather(out_grad, BOTH, axis=0, tiled=False)
        x_all = x_all.reshape(feature_shards, rows, features)
        g_all = g_all.reshape(feature_shards, rows, features)
        part, scores, weight_grads = plain(x_all, g_all, weight, w_gate, w_up, w_down)

    part = part.reshape(feature_shards * shards, tok_rows, features)
    token_grad = lax.psum_scatter(part, BOTH, scatter_dimension=0, tiled=True)[0]
    picked = jnp.sum(jnp.where(hit, scores[:, None, :], 0.0), axis=2)
    gate_grad = lax.psum(lax.psum_scatter(picked, "seq", scatter_dimension=0, tiled=True), "expert")
    grad_gate, grad_up, grad_down = weight_grads()
    return token_grad, grad_gate, grad_up, grad_down, gate_grad


def plain(x_all, g_all, weight, w_gate, w_up, w_down):
    chunks, rows, features = x_all.shape
    experts, depth, width = w_gate.shape
    weight = weight.T[:, :, None]
    gate4 = w_gate.reshape(experts, chunks, features, width)
    up4 = w_up.reshape(experts, chunks, features, width)
    down4 = w_down.reshape(experts, width, chunks, features)
    einsum = functools.partial(jnp.einsum, preferred_element_type=F32)
    pre_gate = einsum("crf,ecfh->erh", x_all, gate4)
    pre_up = einsum("crf,ecfh->erh", x_all, up4)
    back = einsum("crf,ehcf->erh", g_all, down4)
    sig = jax.nn.sigmoid(pre_gate)
    act = pre_gate * sig * pre_up
    scores = jnp.sum(act * back, axis=2).T
    scaled = weight * back
    up_grad = (scaled * pre_gate * sig).astype(BF16)
    pre_grad = (scaled * pre_up * sig * (1.0 + pre_gate * (1.0 - sig))).astype(BF16)
    scaled_act = (weight * act).astype(BF16)
    part = einsum("erh,ecfh->crf", pre_grad, gate4) + einsum("erh,ecfh->crf", up_grad, up4)

    def weight_grads():
        return (
            einsum("crf,erh->ecfh", x_all, pre_grad).astype(BF16).reshape(w_gate.shape),
            einsum("crf,erh->ecfh", x_all, up_grad).astype(BF16).reshape(w_up.shape),
            einsum("erh,crf->ehcf", scaled_act, g_all).astype(BF16).reshape(w_down.shape),
        )

    return part.astype(BF16), scores, weight_grads


def solution(mesh):
    in_specs = (
        P(("groups", "seq"), "expert"),
        P(("groups", "seq"), "expert"),
        P("groups", None),
        P("groups", None),
        P("expert", None, "seq"),
        P("expert", None, "seq"),
        P("expert", "seq", None),
    )
    out_specs = (
        P(("groups", "seq"), "expert"),
        P(("groups", "expert"), None, "seq"),
        P(("groups", "expert"), None, "seq"),
        P(("groups", "expert"), "seq", None),
        P(("groups", "seq"), None),
    )
    return jax.shard_map(body, mesh=mesh, in_specs=in_specs, out_specs=out_specs, check_vma=False)
```

```python
import functools

import jax
import jax.numpy as jnp
from jax import lax
from jax.experimental import pallas as pl
from jax.experimental.pallas import tpu as pltpu
from jax.sharding import PartitionSpec as P

BOTH = ("expert", "seq")
VMEM_BYTES = 56 * 1024 * 1024
BF16 = jnp.bfloat16
F32 = jnp.float32


def params(dims):
    return pltpu.CompilerParams(
        vmem_limit_bytes=VMEM_BYTES, dimension_semantics=("arbitrary",) * dims
    )


def cost(flops, moved):
    return pl.CostEstimate(flops=int(flops), bytes_accessed=int(moved), transcendentals=0)


def dot_nn(a, b):
    return lax.dot_general(a, b, (((1,), (0,)), ((), ())), preferred_element_type=F32)


def dot_nt(a, b):
    return lax.dot_general(a, b, (((1,), (1,)), ((), ())), preferred_element_type=F32)


def forward_kernel(
    tokens_ref, grad_ref, gate_ref, up_ref, down_ref, weight_ref,
    x_all_ref, g_all_ref, grads_ref, scaled_act_ref, scores_ref,
    pre_gate_ref, pre_up_ref, back_ref,
    z_send, z_recv, x_send, x_recv, s_send, s_recv, local_sem,
):
    shards = lax.axis_size("seq")
    z = lax.axis_index("seq")
    me = lax.axis_index("expert")
    sib = me + 1 - 2 * lax.rem(me, 2)
    partner = lax.rem(me + 2, 4)
    far = lax.rem(sib + 2, 4)
    tok_rows, features = tokens_ref.shape
    experts, _, width = gate_ref.shape
    own_refs = (tokens_ref, grad_ref)
    all_refs = (x_all_ref, g_all_ref)

    def place(t, chunk, shard):
        return all_refs[t].at[chunk, pl.ds(pl.multiple_of(shard * tok_rows, tok_rows), tok_rows)]

    def remote(src, dst, send, recv, device):
        return pltpu.make_async_remote_copy(
            src_ref=src, dst_ref=dst, send_sem=send, recv_sem=recv,
            device_id=device, device_id_type=pl.DeviceIdType.MESH,
        )

    def source(t, chunk, d):
        return own_refs[t] if (d == 0 and chunk is me) else place(t, chunk, back_by(d))

    def back_by(d):
        return lax.rem(z + shards - d, shards)

    def z_copy(t, d):
        peer = lax.rem(z + d, shards)
        return remote(own_refs[t], place(t, me, z), z_send.at[t, d], z_recv.at[t, d], {"seq": peer})

    def x_copy(t, d):
        return remote(
            source(t, me, d), place(t, me, back_by(d)), x_send.at[t, d], x_recv.at[t, d],
            {"expert": partner},
        )

    def s_copy(t, which, d):
        chunk = (me, partner)[which]
        at = which * shards + d
        return remote(
            source(t, chunk, d), place(t, chunk, back_by(d)), s_send.at[t, at], s_recv.at[t, at],
            {"expert": sib},
        )

    def local(t):
        return pltpu.make_async_copy(own_refs[t], place(t, me, z), local_sem.at[t])

    barrier = pltpu.get_barrier_semaphore()
    for device in [{"expert": sib}, {"expert": partner}] + [
        {"seq": lax.rem(z + d, shards)} for d in range(1, shards)
    ]:
        pl.semaphore_signal(barrier, inc=1, device_id=device, device_id_type=pl.DeviceIdType.MESH)
    pl.semaphore_wait(barrier, shards + 1)

    group = 2 if experts % 2 == 0 else 1
    rows = shards * tok_rows

    def multiply_tokens(chunk, first):
        def step(x_ref, g_ref, u_ref):
            block = pl.program_id(0)
            for i in range(group):
                e = block * group + i
                new_gate = dot_nn(x_ref[...], g_ref[i])
                new_up = dot_nn(x_ref[...], u_ref[i])
                if first:
                    pre_gate_ref[e] = new_gate
                    pre_up_ref[e] = new_up
                else:
                    pre_gate_ref[e] += new_gate
                    pre_up_ref[e] += new_up

        weights = pl.BlockSpec((group, features, width), lambda b: (b, 0, 0))
        at = pl.ds(pl.multiple_of(chunk * features, features), features)
        pltpu.emit_pipeline(
            step,
            grid=(experts // group,),
            in_specs=[pl.BlockSpec((rows, features), lambda b: (0, 0)), weights, weights],
            out_specs=[],
        )(x_all_ref.at[chunk], gate_ref.at[:, at], up_ref.at[:, at])

    def multiply_grads(chunk, first):
        def step(g_ref, d_ref):
            block = pl.program_id(0)
            for i in range(group):
                e = block * group + i
                new = dot_nt(g_ref[...], d_ref[i])
                if first:
                    back_ref[e] = new
                else:
                    back_ref[e] += new

        at = pl.ds(pl.multiple_of(chunk * features, features), features)
        pltpu.emit_pipeline(
            step,
            grid=(experts // group,),
            in_specs=[
                pl.BlockSpec((rows, features), lambda b: (0, 0)),
                pl.BlockSpec((group, width, features), lambda b: (b, 0, 0)),
            ],
            out_specs=[],
        )(g_all_ref.at[chunk], down_ref.at[:, :, at])

    every = range(shards)
    others = range(1, shards)
    for d in others:
        z_copy(0, d).start()
    x_copy(0, 0).start()
    s_copy(0, 0, 0).start()
    x_copy(1, 0).start()
    local(0).start()
    local(1).start()
    for d in others:
        z_copy(0, d).wait_recv()
        x_copy(0, d).start()
        s_copy(0, 0, d).start()
    for d in others:
        z_copy(1, d).start()
    s_copy(1, 0, 0).start()
    local(0).wait()
    local(1).wait()
    multiply_tokens(me, True)
    for d in every:
        s_copy(0, 0, d).wait_recv()
    multiply_tokens(sib, False)
    for d in every:
        x_copy(0, d).wait_recv()
        s_copy(0, 1, d).start()
    multiply_tokens(partner, False)
    for d in every:
        s_copy(0, 1, d).wait_recv()
    multiply_tokens(far, False)
    for d in others:
        z_copy(1, d).wait_recv()
        x_copy(1, d).start()
        s_copy(1, 0, d).start()
    multiply_grads(me, True)
    for d in every:
        s_copy(1, 0, d).wait_recv()
    multiply_grads(sib, False)
    for d in every:
        x_copy(1, d).wait_recv()
        s_copy(1, 1, d).start()
    multiply_grads(partner, False)
    for d in every:
        s_copy(1, 1, d).wait_recv()
    multiply_grads(far, False)

    for e in range(experts):
        pre_gate = pre_gate_ref[e]
        pre_up = pre_up_ref[e]
        back = back_ref[e]
        r = weight_ref[:, e : e + 1]
        sig = jax.nn.sigmoid(pre_gate)
        silu = pre_gate * sig
        act = silu * pre_up
        scores_ref[:, e : e + 1] = jnp.sum(act * back, axis=1, keepdims=True)
        scaled = r * back
        grads_ref[:, e * width : (e + 1) * width] = (
            scaled * pre_up * sig * (1.0 + pre_gate * (1.0 - sig))
        ).astype(BF16)
        at = (experts + e) * width
        grads_ref[:, at : at + width] = (scaled * silu).astype(BF16)
        scaled_act_ref[e * width : (e + 1) * width, :] = (r * act).T.astype(BF16)

    for t in range(2):
        for d in others:
            z_copy(t, d).wait_send()
        for d in every:
            x_copy(t, d).wait_send()
            s_copy(t, 0, d).wait_send()
            s_copy(t, 1, d).wait_send()


def forward(tokens, out_grad, w_gate, w_up, w_down, weight, shards, chunks):
    tok_rows, features = tokens.shape
    rows = shards * tok_rows
    experts, depth, width = w_gate.shape
    any_spec = pl.BlockSpec(memory_space=pl.ANY)
    vmem_spec = pl.BlockSpec(memory_space=pltpu.VMEM)
    gathered = jax.ShapeDtypeStruct((chunks, rows, features), BF16)
    total = pltpu.VMEM((experts, rows, width), F32)
    dma = pltpu.SemaphoreType.DMA
    return pl.pallas_call(
        forward_kernel,
        in_specs=[any_spec] * 5 + [vmem_spec],
        out_specs=[any_spec] * 2 + [vmem_spec] * 3,
        out_shape=[
            gathered,
            gathered,
            jax.ShapeDtypeStruct((rows, 2 * experts * width), BF16),
            jax.ShapeDtypeStruct((experts * width, rows), BF16),
            jax.ShapeDtypeStruct((rows, experts), F32),
        ],
        scratch_shapes=[
            total,
            total,
            total,
            dma((2, shards)),
            dma((2, shards)),
            dma((2, shards)),
            dma((2, shards)),
            dma((2, 2 * shards)),
            dma((2, 2 * shards)),
            dma((2,)),
        ],
        compiler_params=pltpu.CompilerParams(
            vmem_limit_bytes=VMEM_BYTES, collective_id=0, has_side_effects=True
        ),
        cost_estimate=cost(
            6 * rows * depth * width * experts,
            8 * rows * depth + 6 * experts * depth * width,
        ),
        name="forward",
    )(tokens, out_grad, w_gate, w_up, w_down, weight)


def row_kernel(ids_ref, grads_ref, gate_ref, up_ref, out_ref):
    experts, _, width = gate_ref.shape
    total = None
    for e in range(experts):
        for half, ref in enumerate((gate_ref, up_ref)):
            at = (half * experts + e) * width
            term = dot_nt(grads_ref[:, at : at + width], ref[e])
            total = term if total is None else total + term
    out_ref[0] = total.astype(BF16)


def row_products(grads, w_gate, w_up, ids, features, steps):
    rows = grads.shape[0]
    experts, depth, width = w_gate.shape
    count = ids.shape[0]
    cut = features // steps
    weight_spec = pl.BlockSpec((experts, cut, width), lambda c, n, ids: (0, ids[c] * steps + n, 0))
    return pl.pallas_call(
        row_kernel,
        grid_spec=pltpu.PrefetchScalarGridSpec(
            num_scalar_prefetch=1,
            grid=(count, steps),
            in_specs=[
                pl.BlockSpec(grads.shape, lambda c, n, ids: (0, 0)),
                weight_spec,
                weight_spec,
            ],
            out_specs=pl.BlockSpec((1, rows, cut), lambda c, n, ids: (c, 0, n)),
        ),
        out_shape=jax.ShapeDtypeStruct((count, rows, features), BF16),
        compiler_params=params(2),
        cost_estimate=cost(
            4 * rows * count * features * width * experts,
            2 * rows * count * features + 4 * experts * count * features * width,
        ),
        name="row_products",
    )(ids, grads, w_gate, w_up)


def tall_kernel(x_ref, grads_ref, out_ref):
    experts, _, width = out_ref.shape
    x_t = x_ref[0].T
    for e in range(experts):
        out_ref[e] = dot_nn(x_t, grads_ref[:, e * width : (e + 1) * width]).astype(BF16)


def wide_kernel(g_ref, act_ref, out_ref):
    experts, width, _ = out_ref.shape
    for e in range(experts):
        out_ref[e] = dot_nn(act_ref[e * width : (e + 1) * width, :], g_ref[0]).astype(BF16)


def weight_products(kernel, source, factor, factor_shape, half, out_shape, tall, steps):
    chunks, rows, features = source.shape
    cut = features // steps
    experts = out_shape[0]
    if tall:
        out_spec = pl.BlockSpec((experts, cut, out_shape[2]), lambda c, n: (0, c * steps + n, 0))
    else:
        out_spec = pl.BlockSpec((experts, out_shape[1], cut), lambda c, n: (0, 0, c * steps + n))
    size = out_shape[0] * out_shape[1] * out_shape[2]
    return pl.pallas_call(
        kernel,
        grid=(chunks, steps),
        in_specs=[
            pl.BlockSpec((1, rows, cut), lambda c, n: (c, 0, n)),
            pl.BlockSpec(factor_shape, lambda c, n: (0, half)),
        ],
        out_specs=out_spec,
        out_shape=jax.ShapeDtypeStruct(out_shape, BF16),
        compiler_params=params(2),
        cost_estimate=cost(2 * rows * size, 2 * rows * chunks * features + 2 * size),
        name="weight_products",
    )(source, factor)


def scatter_rows(grads, w_gate, w_up, features, shards, tok_rows):
    me = lax.axis_index("expert")
    z = lax.axis_index("seq")
    sib = me + 1 - 2 * (me % 2)
    partner, far = (me + 2) % 4, (sib + 2) % 4
    to_sib = [(i, i ^ 1) for i in range(4)]
    to_partner = [(i, (i + 2) % 4) for i in range(4)]
    sent = row_products(grads, w_gate, w_up, jnp.stack([far, sib]), features, 2)
    first = lax.ppermute(sent[0], "expert", to_sib)
    second = lax.ppermute(sent[1], "expert", to_sib)
    kept = row_products(grads, w_gate, w_up, jnp.stack([partner, me]), features, 2)

    def cut(array, d):
        return lax.dynamic_slice_in_dim(array, (z + d) % shards * tok_rows, tok_rows, 0)

    total = None
    for d in [*range(1, shards), 0]:
        there = cut(kept[0], d).astype(F32) + cut(first, d).astype(F32)
        there = lax.ppermute(there.astype(BF16), "expert", to_partner)
        here = cut(kept[1], d).astype(F32) + cut(second, d).astype(F32) + there.astype(F32)
        if d:
            along = [(i, (i + d) % shards) for i in range(shards)]
            here = lax.ppermute(here.astype(BF16), "seq", along).astype(F32)
        total = here if total is None else total + here
    return total.astype(BF16)


def body(tokens, out_grad, routes, route_weights, w_gate, w_up, w_down):
    shards = lax.axis_size("seq")
    feature_shards = lax.axis_size("expert")
    tok_rows, features = tokens.shape
    rows = shards * tok_rows
    local_experts, depth, width = w_gate.shape
    first_expert = lax.axis_index("expert") * local_experts

    local_ids = first_expert + jnp.arange(local_experts, dtype=jnp.int32)
    hit = routes[:, :, None] == local_ids[None, None, :]
    weight = jnp.sum(jnp.where(hit, route_weights[:, :, None], 0.0), axis=1)

    if feature_shards == 4 and features % 256 == 0:
        x_all, g_all, grads, act_t, scores = forward(
            tokens, out_grad, w_gate, w_up, w_down, weight, shards, feature_shards
        )
        token_grad = scatter_rows(grads, w_gate, w_up, features, shards, tok_rows)
        half = (rows, local_experts * width)

        def weight_grads():
            return (
                weight_products(tall_kernel, x_all, grads, half, 0, w_gate.shape, True, 2),
                weight_products(tall_kernel, x_all, grads, half, 1, w_up.shape, True, 2),
                weight_products(wide_kernel, g_all, act_t, act_t.shape, 0, w_down.shape, False, 2),
            )

    else:
        x_all = lax.all_gather(tokens, BOTH, axis=0, tiled=False)
        g_all = lax.all_gather(out_grad, BOTH, axis=0, tiled=False)
        x_all = x_all.reshape(feature_shards, rows, features)
        g_all = g_all.reshape(feature_shards, rows, features)
        part, scores, weight_grads = plain(x_all, g_all, weight, w_gate, w_up, w_down)
        part = part.reshape(feature_shards * shards, tok_rows, features)
        token_grad = lax.psum_scatter(part, BOTH, scatter_dimension=0, tiled=True)[0]

    picked = jnp.sum(jnp.where(hit, scores[:, None, :], 0.0), axis=2)
    gate_grad = lax.psum(lax.psum_scatter(picked, "seq", scatter_dimension=0, tiled=True), "expert")
    grad_gate, grad_up, grad_down = weight_grads()
    return token_grad, grad_gate, grad_up, grad_down, gate_grad


def plain(x_all, g_all, weight, w_gate, w_up, w_down):
    chunks, rows, features = x_all.shape
    experts, depth, width = w_gate.shape
    weight = weight.T[:, :, None]
    gate4 = w_gate.reshape(experts, chunks, features, width)
    up4 = w_up.reshape(experts, chunks, features, width)
    down4 = w_down.reshape(experts, width, chunks, features)
    einsum = functools.partial(jnp.einsum, preferred_element_type=F32)
    pre_gate = einsum("crf,ecfh->erh", x_all, gate4)
    pre_up = einsum("crf,ecfh->erh", x_all, up4)
    back = einsum("crf,ehcf->erh", g_all, down4)
    sig = jax.nn.sigmoid(pre_gate)
    act = pre_gate * sig * pre_up
    scores = jnp.sum(act * back, axis=2).T
    scaled = weight * back
    up_grad = (scaled * pre_gate * sig).astype(BF16)
    pre_grad = (scaled * pre_up * sig * (1.0 + pre_gate * (1.0 - sig))).astype(BF16)
    scaled_act = (weight * act).astype(BF16)
    part = einsum("erh,ecfh->crf", pre_grad, gate4) + einsum("erh,ecfh->crf", up_grad, up4)

    def weight_grads():
        return (
            einsum("crf,erh->ecfh", x_all, pre_grad).astype(BF16).reshape(w_gate.shape),
            einsum("crf,erh->ecfh", x_all, up_grad).astype(BF16).reshape(w_up.shape),
            einsum("erh,crf->ehcf", scaled_act, g_all).astype(BF16).reshape(w_down.shape),
        )

    return part.astype(BF16), scores, weight_grads


def solution(mesh):
    in_specs = (
        P(("groups", "seq"), "expert"),
        P(("groups", "seq"), "expert"),
        P("groups", None),
        P("groups", None),
        P("expert", None, "seq"),
        P("expert", None, "seq"),
        P("expert", "seq", None),
    )
    out_specs = (
        P(("groups", "seq"), "expert"),
        P(("groups", "expert"), None, "seq"),
        P(("groups", "expert"), None, "seq"),
        P(("groups", "expert"), "seq", None),
        P(("groups", "seq"), None),
    )
    return jax.shard_map(body, mesh=mesh, in_specs=in_specs, out_specs=out_specs, check_vma=False)
```
